32 devices in a mesh: shard: 4 (over x, core), tensor: 8 (over z, y).
Axes of the slice: x: 2, y: 2, z: 4, core: 2. Of those that a mesh axis runs over, the one named last changes fastest.
Arguments:
- grad_square: bfloat16 [4, 768, 768], P(None, 'shard'), may hold values from -64 to 64
- grad_wide: bfloat16 [4, 2048, 768], P(None, 'shard'), may hold values from -64 to 64
- moment_square: float32 [4, 589824], P(None, ('shard', 'tensor')), may hold values from -6 to 6
- moment_wide: float32 [4, 1572864], P(None, ('shard', 'tensor')), may hold values from -6 to 6
Outputs:
- update_square: float32 [4, 768, 768], P(None, 'shard')
- update_wide: float32 [4, 2048, 768], P(None, 'shard')
- new_moment_square: float32 [4, 589824], P(None, ('shard', 'tensor'))
- new_moment_wide: float32 [4, 1572864], P(None, ('shard', 'tensor'))
The draws below stay inside these ranges and needn't reach their ends.
All inputs are finite; a program needn't handle non-finite values.
Results may differ from the reference program's by a relative error of at most 0.0003.
Values sent between devices are 32-bit elements; how exact they have to be, the bound alone decides.
A program may use at most 128 MiB of HBM per device.

```python
import math
import jax
import jax.numpy as jnp
from jax import lax

D = 768
FF = 2048
ITERS = 3
NSQ = 4
NW = 4


def scaled_draw(key, matrix_count, row_count, columns):
    key_noise, key_row, key_col = jax.random.split(key, 3)
    position = jnp.arange(row_count, dtype=jnp.float32) / float(row_count - 1)
    rising = jnp.exp((position - 1.0) * math.log(3.0))[None, :, None]
    noise = jnp.clip(jax.random.normal(key_noise, (matrix_count, row_count, columns), jnp.float32), -6.0, 6.0)
    half_range = 0.5 * math.log(10.0)
    row_scale = jnp.exp(jax.random.uniform(key_row, (matrix_count, row_count, 1), jnp.float32, -half_range, half_range))
    col_scale = jnp.exp(jax.random.uniform(key_col, (matrix_count, 1, columns), jnp.float32, -half_range, half_range))
    return noise * row_scale * col_scale * rising


def draw_grad_square(key, part):
    return scaled_draw(jax.random.fold_in(key, 11), NSQ, D, D).astype(jnp.bfloat16)


def draw_grad_wide(key, part):
    return scaled_draw(jax.random.fold_in(key, 23), NW, FF, D).astype(jnp.bfloat16)


def block_scale(stream_key, extent, cuts, least, largest):
    level = 1.0
    for dim, blocks in cuts:
        steps = jax.random.uniform(jax.random.fold_in(jax.random.fold_in(stream_key, 6), dim), (blocks,), jnp.float32, least / len(cuts), largest / len(cuts))
        level = level * jnp.repeat(jnp.exp(steps), extent[dim] // blocks).reshape((-1,) + (1,) * (len(extent) - 1 - dim))
    return level


def bell_draw(stream_key, shape, deviation, bound, cuts=(), kind=jnp.bfloat16):
    level = block_scale(stream_key, shape, cuts, -0.22, 0.18) if cuts else 1.0
    array = jax.random.normal(stream_key, shape, jnp.float32) * deviation * level
    return jnp.minimum(jnp.maximum(array, -bound), bound).astype(kind)


def setup_inputs(seed: int = 0) -> dict:
    keys = jax.random.split(jax.random.key(seed), 5)
    return {
        "grad_square": draw_grad_square(jax.random.fold_in(keys[4], 71), 0),
        "grad_wide": draw_grad_wide(jax.random.fold_in(keys[4], 71), 0),
        "moment_square": bell_draw(keys[2], (NSQ, D * D), 1.0, 6.0, ((1, 32),), jnp.float32),
        "moment_wide": bell_draw(keys[3], (NW, FF * D), 1.0, 6.0, ((1, 32),), jnp.float32),
    }


coef_a = 3.4445
coef_b = -4.775
coef_c = 2.0315
momentum_decay = 0.95
epsilon = 1e-07

def orthogonalize(look):
    row_total = look.shape[0]
    current = look / (jnp.sqrt(jnp.sum(look * look)) + epsilon)
    for iteration in range(ITERS):
        gram = jnp.dot(current.T, current, precision=lax.Precision.HIGHEST, preferred_element_type=jnp.float32)
        square_gram = jnp.dot(gram, gram, precision=lax.Precision.HIGHEST, preferred_element_type=jnp.float32)
        mixer = coef_b * gram + coef_c * square_gram
        product = jnp.dot(current, mixer, precision=lax.Precision.HIGHEST, preferred_element_type=jnp.float32)
        current = coef_a * current + product
    return math.sqrt(row_total) * current

def advance(grad, moment):
    grad_float = grad.astype(jnp.float32)
    new_moment = momentum_decay * moment.reshape(grad.shape) + grad_float
    look = grad_float + momentum_decay * new_moment
    update = lax.map(orthogonalize, look)
    return (update, new_moment.reshape(moment.shape))

def reference(grad_square, grad_wide, moment_square, moment_wide):
    update_square, new_moment_square = advance(grad_square, moment_square)
    update_wide, new_moment_wide = advance(grad_wide, moment_wide)
    return (update_square, update_wide, new_moment_square, new_moment_wide)
```

```python
import math

import jax
import jax.numpy as jnp
from jax import lax
from jax.sharding import PartitionSpec as P

ITERS = 3

coef_a = 3.4445
coef_b = -4.775
coef_c = 2.0315
momentum_decay = 0.95
epsilon = 1e-07


def dot(a, b):
    return jnp.dot(
        a, b, precision=lax.Precision.HIGH, preferred_element_type=jnp.float32
    )


def dot_rows(a, b):
    return lax.dot_general(
        a,
        b,
        (((0,), (0,)), ((), ())),
        precision=lax.Precision.HIGH,
        preferred_element_type=jnp.float32,
    )


def own_rows(grad, member, tensor_count):
    row_piece = grad.shape[1] // tensor_count
    return lax.dynamic_slice_in_dim(grad, member * row_piece, row_piece, 1)


def summed_gram(rows, shard_count):
    width = rows.shape[1]
    b = width // 3
    left, middle, right = rows[:, :b], rows[:, b : 2 * b], rows[:, 2 * b :]
    half_0 = dot_rows(left, rows)
    half_1 = jnp.concatenate(
        [dot_rows(middle, rows[:, b:]), dot_rows(right, right)], axis=1
    )
    first = lax.axis_index("shard") % 2 == 0
    across = [(i, i ^ 1) for i in range(shard_count)]
    kept = jnp.where(first, half_0, half_1)
    sent = jnp.where(first, half_1, half_0)
    pair = kept + lax.ppermute(sent, "shard", across)
    total = pair
    for hop in range(1, shard_count // 2):
        along = [(i, (i + 2 * hop) % shard_count) for i in range(shard_count)]
        total = total + lax.ppermute(pair, "shard", along)
    other = lax.ppermute(total, "shard", across)
    half_0 = jnp.where(first, total, other)
    half_1 = jnp.where(first, other, total)
    g01, g02 = half_0[:, b : 2 * b], half_0[:, 2 * b :]
    g12 = half_1[:, b : 2 * b]
    row_1 = jnp.concatenate([g01.T, half_1[:, : 2 * b]], axis=1)
    row_2 = jnp.concatenate([g02.T, g12.T, half_1[:, 2 * b :]], axis=1)
    return jnp.concatenate([half_0, row_1, row_2], axis=0)


def shards(grad_square, grad_wide, moment_square, moment_wide):
    tensor_count = lax.axis_size("tensor")
    shard_count = lax.axis_size("shard")
    member = lax.axis_index("tensor")
    matrices, rows_square, width = grad_square.shape
    rows_wide = grad_wide.shape[1]
    piece_square = rows_square // tensor_count
    piece_wide = rows_wide // tensor_count
    flat_square = own_rows(grad_square, member, tensor_count).astype(jnp.float32)
    flat_wide = own_rows(grad_wide, member, tensor_count).astype(jnp.float32)
    new_square = momentum_decay * moment_square.reshape(flat_square.shape) + flat_square
    new_wide = momentum_decay * moment_wide.reshape(flat_wide.shape) + flat_wide
    look_square = flat_square + momentum_decay * new_square
    look_wide = flat_wide + momentum_decay * new_wide

    padded = jnp.pad(look_square, ((0, 0), (0, piece_wide - piece_square), (0, 0)))
    dealt = jnp.stack([padded, look_wide], axis=1).reshape(
        tensor_count, piece_wide, width
    )
    held = lax.all_to_all(dealt, "tensor", split_axis=0, concat_axis=0, tiled=True)
    current = held.reshape(rows_wide, width)

    is_wide = member % 2 == 1
    gram = summed_gram(current, shard_count)
    eye = jnp.eye(width, dtype=jnp.float32)
    total = jnp.sum(gram * eye)
    scale = 1.0 / (jnp.sqrt(total) + epsilon)
    gram = gram * (scale * scale)
    current = current * scale
    for iteration in range(ITERS):
        mixer = coef_b * gram + coef_c * dot(gram, gram)
        current = coef_a * current + dot(current, mixer)
        if iteration < ITERS - 1:
            mixed = coef_a * gram + dot(gram, mixer)
            gram = coef_a * mixed + dot(mixed, mixer)
    row_total = jnp.where(
        is_wide,
        math.sqrt(rows_wide * shard_count),
        math.sqrt(rows_square * shard_count),
    ).astype(jnp.float32)
    current = row_total * current

    even = (rows_square + rows_wide) // 2
    short = current.reshape(tensor_count, piece_wide, width)[:, :piece_square]
    moved = lax.ppermute(
        current[even:], "tensor", [(2 * k + 1, 2 * k) for k in range(tensor_count // 2)]
    )
    mine = jnp.where(
        is_wide,
        current[:even],
        jnp.concatenate([short.reshape(rows_square, width), moved], axis=0),
    )
    gathered = lax.all_gather(mine, "tensor", axis=0, tiled=True).reshape(
        matrices, 2, even, width
    )
    update_square = gathered[:, 0, :rows_square]
    update_wide = jnp.concatenate(
        [gathered[:, 1], gathered[:, 0, rows_square:]], axis=1
    )
    return (
        update_square,
        update_wide,
        new_square.reshape(moment_square.shape),
        new_wide.reshape(moment_wide.shape),
    )


def solution(mesh):
    in_specs = (
        P(None, "shard", None),
        P(None, "shard", None),
        P(None, ("shard", "tensor")),
        P(None, ("shard", "tensor")),
    )
    return jax.shard_map(
        shards, mesh=mesh, in_specs=in_specs, out_specs=in_specs, check_vma=False
    )
```

```python
import functools
import math

import jax
import jax.numpy as jnp
from jax import lax
from jax.experimental import pallas as pl
from jax.experimental.pallas import tpu as pltpu
from jax.sharding import PartitionSpec as P

ITERS = 3
LAYERS = 4
CHUNKS = 4

coef_a = 3.4445
coef_b = -4.775
coef_c = 2.0315
momentum_decay = 0.95
epsilon = 1e-07


def dot(a, b):
    return jnp.dot(
        a, b, precision=lax.Precision.HIGH, preferred_element_type=jnp.float32
    )


def dot_rows(a, b):
    return lax.dot_general(
        a,
        b,
        (((0,), (0,)), ((), ())),
        precision=lax.Precision.HIGH,
        preferred_element_type=jnp.float32,
    )


def own_rows(grad, member, tensor_count):
    row_piece = grad.shape[1] // tensor_count
    return lax.dynamic_slice_in_dim(grad, member * row_piece, row_piece, 1)


def summed_gram(rows, shard_count):
    width = rows.shape[1]
    b = width // 3
    left, middle, right = rows[:, :b], rows[:, b : 2 * b], rows[:, 2 * b :]
    half_0 = dot_rows(left, rows)
    half_1 = jnp.concatenate(
        [dot_rows(middle, rows[:, b:]), dot_rows(right, right)], axis=1
    )
    first = lax.axis_index("shard") % 2 == 0
    across = [(i, i ^ 1) for i in range(shard_count)]
    kept = jnp.where(first, half_0, half_1)
    sent = jnp.where(first, half_1, half_0)
    pair = kept + lax.ppermute(sent, "shard", across)
    total = pair
    for hop in range(1, shard_count // 2):
        along = [(i, (i + 2 * hop) % shard_count) for i in range(shard_count)]
        total = total + lax.ppermute(pair, "shard", along)
    other = lax.ppermute(total, "shard", across)
    half_0 = jnp.where(first, total, other)
    half_1 = jnp.where(first, other, total)
    g01, g02 = half_0[:, b : 2 * b], half_0[:, 2 * b :]
    g12 = half_1[:, b : 2 * b]
    row_1 = jnp.concatenate([g01.T, half_1[:, : 2 * b]], axis=1)
    row_2 = jnp.concatenate([g02.T, g12.T, half_1[:, 2 * b :]], axis=1)
    return jnp.concatenate([half_0, row_1, row_2], axis=0)


def spread(layers, columns, x_ref, square_ref, wide_ref, local_sem, send_sem, recv_sem):
    me = lax.axis_index("tensor")
    shard = lax.axis_index("shard")
    layer = me // columns
    column = me % columns
    blocks = (square_ref, wide_ref)

    def device(to_layer, to_column):
        return (shard, to_layer * columns + to_column)

    def sideways(step):
        return lax.rem(column + step, columns)

    has_next = layer < layers - 1
    has_last = layer > 0
    barrier = pltpu.get_barrier_semaphore()

    def greet(target):
        pl.semaphore_signal(
            barrier, inc=1, device_id=target, device_id_type=pl.DeviceIdType.MESH
        )

    for step in range(1, columns):
        greet(device(layer, sideways(step)))

    @pl.when(has_next)
    def _():
        greet(device(layer + 1, column))

    @pl.when(has_last)
    def _():
        greet(device(layer - 1, column))

    pl.semaphore_wait(
        barrier, columns - 1 + has_next.astype(jnp.int32) + has_last.astype(jnp.int32)
    )

    def slot(kind, from_layer, from_column, chunk):
        block = blocks[kind]
        rows = block.shape[1] // CHUNKS
        return block.at[
            (from_layer * columns + from_column) // 2, pl.ds(chunk * rows, rows)
        ]

    def copy(kind, from_layer, from_column, chunk, way, target, source=None):
        place = slot(kind, from_layer, from_column, chunk)
        index = from_layer * columns + from_column
        return pltpu.make_async_remote_copy(
            src_ref=place if source is None else source,
            dst_ref=place,
            send_sem=send_sem.at[index, chunk, way],
            recv_sem=recv_sem.at[index, chunk],
            device_id=target,
            device_id_type=pl.DeviceIdType.MESH,
        )

    def routes(kind, distance, sign, chunk, act):
        origin = layer + sign * distance
        source = None
        if distance == 0:
            rows = blocks[kind].shape[1] // CHUNKS
            source = x_ref.at[pl.ds(chunk * rows, rows)]
        if distance == 0 or sign < 0:

            @pl.when(has_next)
            def _():
                act(copy(kind, origin, column, chunk, 0, device(layer + 1, column), source))

        if distance == 0 or sign > 0:

            @pl.when(has_last)
            def _():
                act(copy(kind, origin, column, chunk, 1, device(layer - 1, column), source))

        for step in range(1, columns):
            act(
                copy(
                    kind, origin, column, chunk, 1 + step,
                    device(layer, sideways(step)), source,
                )
            )

    def visit(act, arrive):
        for distance in range(layers):
            for kind in (0, 1):

                @pl.when(lax.rem(column + layer + distance, 2) == kind)
                def _():
                    for chunk in range(CHUNKS):
                        for sign in (-1, 1) if distance else (1,):
                            origin = layer + sign * distance

                            @pl.when((origin >= 0) & (origin < layers))
                            def _():
                                if distance and arrive:
                                    copy(
                                        kind, origin, column, chunk, 0,
                                        device(layer, sideways(1)),
                                    ).wait_recv()
                                routes(kind, distance, sign, chunk, act)

    visit(lambda c: c.start(), True)
    for kind in (0, 1):

        @pl.when(lax.rem(column + layer, 2) == kind)
        def _():
            block = blocks[kind]
            local = pltpu.make_async_copy(
                x_ref.at[pl.ds(0, block.shape[1])], block.at[me // 2], local_sem
            )
            local.start()
            local.wait()

    visit(lambda c: c.wait_send(), False)
    for origin in range(layers):
        for step in range(1, columns):
            for kind in (0, 1):

                @pl.when(lax.rem(sideways(step) + origin, 2) == kind)
                def _():
                    for chunk in range(CHUNKS):
                        copy(
                            kind, origin, sideways(step), chunk, 0,
                            device(layer, sideways(1)),
                        ).wait_recv()


def gather_rows(rows, matrices, rows_square, rows_wide, tensor_count):
    width = rows.shape[1]
    columns = tensor_count // LAYERS
    return pl.pallas_call(
        functools.partial(spread, LAYERS, columns),
        out_shape=(
            jax.ShapeDtypeStruct((matrices, rows_square, width), jnp.float32),
            jax.ShapeDtypeStruct((matrices, rows_wide, width), jnp.float32),
        ),
        in_specs=[pl.BlockSpec(memory_space=pl.ANY)],
        out_specs=(
            pl.BlockSpec(memory_space=pl.ANY),
            pl.BlockSpec(memory_space=pl.ANY),
        ),
        scratch_shapes=[
            pltpu.SemaphoreType.DMA,
            pltpu.SemaphoreType.DMA((tensor_count, CHUNKS, 1 + columns)),
            pltpu.SemaphoreType.DMA((tensor_count, CHUNKS)),
        ],
        compiler_params=pltpu.CompilerParams(collective_id=0, has_side_effects=True),
    )(rows)


def shards(grad_square, grad_wide, moment_square, moment_wide):
    tensor_count = lax.axis_size("tensor")
    shard_count = lax.axis_size("shard")
    member = lax.axis_index("tensor")
    matrices, rows_square, width = grad_square.shape
    rows_wide = grad_wide.shape[1]
    piece_square = rows_square // tensor_count
    piece_wide = rows_wide // tensor_count
    flat_square = own_rows(grad_square, member, tensor_count).astype(jnp.float32)
    flat_wide = own_rows(grad_wide, member, tensor_count).astype(jnp.float32)
    new_square = momentum_decay * moment_square.reshape(flat_square.shape) + flat_square
    new_wide = momentum_decay * moment_wide.reshape(flat_wide.shape) + flat_wide
    look_square = flat_square + momentum_decay * new_square
    look_wide = flat_wide + momentum_decay * new_wide

    columns = tensor_count // LAYERS
    padded = jnp.pad(look_square, ((0, 0), (0, piece_wide - piece_square), (0, 0)))
    dealt = jnp.stack(
        [
            (look_wide if (t // columns + t % columns) % 2 else padded)[t // 2]
            for t in range(tensor_count)
        ]
    )
    held = lax.all_to_all(dealt, "tensor", split_axis=0, concat_axis=0, tiled=True)
    is_wide = (member // columns + member % columns) % 2 == 1
    current = held.reshape(rows_wide, width)
    short = held[:, :piece_square].reshape(rows_square, width)
    gram = summed_gram(current, shard_count)
    eye = jnp.eye(width, dtype=jnp.float32)
    total = jnp.sum(gram * eye)
    scale = 1.0 / (jnp.sqrt(total) + epsilon)
    gram = gram * (scale * scale)
    current = scale * jnp.where(
        is_wide, current, jnp.pad(short, ((0, rows_wide - rows_square), (0, 0)))
    )
    for iteration in range(ITERS):
        mixer = coef_b * gram + coef_c * dot(gram, gram)
        current = coef_a * current + dot(current, mixer)
        if iteration < ITERS - 1:
            mixed = coef_a * gram + dot(gram, mixer)
            gram = coef_a * mixed + dot(mixed, mixer)
    row_total = jnp.where(
        is_wide,
        math.sqrt(rows_wide * shard_count),
        math.sqrt(rows_square * shard_count),
    ).astype(jnp.float32)
    current = row_total * current

    update_square, update_wide = gather_rows(
        current, matrices, rows_square, rows_wide, tensor_count
    )
    return (
        update_square,
        update_wide,
        new_square.reshape(moment_square.shape),
        new_wide.reshape(moment_wide.shape),
    )


def solution(mesh):
    in_specs = (
        P(None, "shard", None),
        P(None, "shard", None),
        P(None, ("shard", "tensor")),
        P(None, ("shard", "tensor")),
    )
    return jax.shard_map(
        shards, mesh=mesh, in_specs=in_specs, out_specs=in_specs, check_vma=False
    )
```

```python
import functools
import math

import jax
import jax.numpy as jnp
from jax import lax
from jax.experimental import pallas as pl
from jax.experimental.pallas import tpu as pltpu
from jax.sharding import PartitionSpec as P

ITERS = 3
LAYERS = 4
CHUNKS = 4

coef_a = 3.4445
coef_b = -4.775
coef_c = 2.0315
momentum_decay = 0.95
epsilon = 1e-07


def dot(a, b):
    return jnp.dot(
        a, b, precision=lax.Precision.HIGH, preferred_element_type=jnp.float32
    )


def dot_rows(a, b):
    return lax.dot_general(
        a,
        b,
        (((0,), (0,)), ((), ())),
        precision=lax.Precision.HIGH,
        preferred_element_type=jnp.float32,
    )


def own_rows(grad, member, tensor_count):
    row_piece = grad.shape[1] // tensor_count
    return lax.dynamic_slice_in_dim(grad, member * row_piece, row_piece, 1)


def summed_gram(rows, shard_count):
    width = rows.shape[1]
    b = width // 3
    left, middle, right = rows[:, :b], rows[:, b : 2 * b], rows[:, 2 * b :]
    half_0 = dot_rows(left, rows)
    half_1 = jnp.concatenate(
        [dot_rows(middle, rows[:, b:]), dot_rows(right, right)], axis=1
    )
    first = lax.axis_index("shard") % 2 == 0
    across = [(i, i ^ 1) for i in range(shard_count)]
    kept = jnp.where(first, half_0, half_1)
    sent = jnp.where(first, half_1, half_0)
    pair = kept + lax.ppermute(sent, "shard", across)
    total = pair
    for hop in range(1, shard_count // 2):
        along = [(i, (i + 2 * hop) % shard_count) for i in range(shard_count)]
        total = total + lax.ppermute(pair, "shard", along)
    other = lax.ppermute(total, "shard", across)
    half_0 = jnp.where(first, total, other)
    half_1 = jnp.where(first, other, total)
    g01, g02 = half_0[:, b : 2 * b], half_0[:, 2 * b :]
    g12 = half_1[:, b : 2 * b]
    row_1 = jnp.concatenate([g01.T, half_1[:, : 2 * b]], axis=1)
    row_2 = jnp.concatenate([g02.T, g12.T, half_1[:, 2 * b :]], axis=1)
    return jnp.concatenate([half_0, row_1, row_2], axis=0)


def spread(layers, columns, x_ref, square_ref, wide_ref, local_sem, send_sem, recv_sem):
    me = lax.axis_index("tensor")
    shard = lax.axis_index("shard")
    layer = me // columns
    column = me % columns
    blocks = (square_ref, wide_ref)

    def device(to_layer, to_column):
        return (shard, to_layer * columns + to_column)

    def sideways(step):
        return lax.rem(column + step, columns)

    has_next = layer < layers - 1
    has_last = layer > 0
    barrier = pltpu.get_barrier_semaphore()

    def greet(target):
        pl.semaphore_signal(
            barrier, inc=1, device_id=target, device_id_type=pl.DeviceIdType.MESH
        )

    for step in range(1, columns):
        greet(device(layer, sideways(step)))

    @pl.when(has_next)
    def _():
        greet(device(layer + 1, column))

    @pl.when(has_last)
    def _():
        greet(device(layer - 1, column))

    pl.semaphore_wait(
        barrier, columns - 1 + has_next.astype(jnp.int32) + has_last.astype(jnp.int32)
    )

    def slot(kind, from_layer, from_column, chunk):
        block = blocks[kind]
        rows = block.shape[1] // CHUNKS
        return block.at[
            (from_layer * columns + from_column) // 2, pl.ds(chunk * rows, rows)
        ]

    def copy(kind, from_layer, from_column, chunk, way, target, source=None):
        place = slot(kind, from_layer, from_column, chunk)
        index = from_layer * columns + from_column
        return pltpu.make_async_remote_copy(
            src_ref=place if source is None else source,
            dst_ref=place,
            send_sem=send_sem.at[index, chunk, way],
            recv_sem=recv_sem.at[index, chunk],
            device_id=target,
            device_id_type=pl.DeviceIdType.MESH,
        )

    def routes(kind, distance, sign, chunk, act):
        origin = layer + sign * distance
        source = None
        if distance == 0:
            rows = blocks[kind].shape[1] // CHUNKS
            source = x_ref.at[pl.ds(chunk * rows, rows)]
        if distance == 0 or sign < 0:

            @pl.when(has_next)
            def _():
                act(copy(kind, origin, column, chunk, 0, device(layer + 1, column), source))

        if distance == 0 or sign > 0:

            @pl.when(has_last)
            def _():
                act(copy(kind, origin, column, chunk, 1, device(layer - 1, column), source))

        for step in range(1, columns):
            act(
                copy(
                    kind, origin, column, chunk, 1 + step,
                    device(layer, sideways(step)), source,
                )
            )

    def visit(act, arrive):
        for distance in range(layers):
            for kind in (0, 1):

                @pl.when(lax.rem(column + layer + distance, 2) == kind)
                def _():
                    for chunk in range(CHUNKS):
                        for sign in (-1, 1) if distance else (1,):
                            origin = layer + sign * distance

                            @pl.when((origin >= 0) & (origin < layers))
                            def _():
                                if distance and arrive:
                                    copy(
                                        kind, origin, column, chunk, 0,
                                        device(layer, sideways(1)),
                                    ).wait_recv()
                                routes(kind, distance, sign, chunk, act)

    visit(lambda c: c.start(), True)
    for kind in (0, 1):

        @pl.when(lax.rem(column + layer, 2) == kind)
        def _():
            block = blocks[kind]
            local = pltpu.make_async_copy(
                x_ref.at[pl.ds(0, block.shape[1])], block.at[me // 2], local_sem
            )
            local.start()
            local.wait()

    visit(lambda c: c.wait_send(), False)
    for origin in range(layers):
        for step in range(1, columns):
            for kind in (0, 1):

                @pl.when(lax.rem(sideways(step) + origin, 2) == kind)
                def _():
                    for chunk in range(CHUNKS):
                        copy(
                            kind, origin, sideways(step), chunk, 0,
                            device(layer, sideways(1)),
                        ).wait_recv()


def gather_rows(rows, matrices, rows_square, rows_wide, tensor_count):
    width = rows.shape[1]
    columns = tensor_count // LAYERS
    return pl.pallas_call(
        functools.partial(spread, LAYERS, columns),
        out_shape=(
            jax.ShapeDtypeStruct((matrices, rows_square, width), jnp.float32),
            jax.ShapeDtypeStruct((matrices, rows_wide, width), jnp.float32),
        ),
        in_specs=[pl.BlockSpec(memory_space=pl.ANY)],
        out_specs=(
            pl.BlockSpec(memory_space=pl.ANY),
            pl.BlockSpec(memory_space=pl.ANY),
        ),
        scratch_shapes=[
            pltpu.SemaphoreType.DMA,
            pltpu.SemaphoreType.DMA((tensor_count, CHUNKS, 1 + columns)),
            pltpu.SemaphoreType.DMA((tensor_count, CHUNKS)),
        ],
        compiler_params=pltpu.CompilerParams(collective_id=0, has_side_effects=True),
    )(rows)


def deal(
    columns, tensor_count, look_square, look_wide, held_square, held_wide,
    local_sem, send_sem, recv_sem,
):
    me = lax.axis_index("tensor")
    shard = lax.axis_index("shard")
    looks = (look_square, look_wide)
    helds = (held_square, held_wide)
    barrier = pltpu.get_barrier_semaphore()

    def takes(member):
        return lax.rem(member // columns + lax.rem(member, columns), 2)

    for step in range(1, tensor_count):
        pl.semaphore_signal(
            barrier,
            inc=1,
            device_id=(shard, lax.rem(me + step, tensor_count)),
            device_id_type=pl.DeviceIdType.MESH,
        )
    pl.semaphore_wait(barrier, tensor_count - 1)

    def copy(kind, target, source):
        return pltpu.make_async_remote_copy(
            src_ref=looks[kind].at[target // 2],
            dst_ref=helds[kind].at[source],
            send_sem=send_sem.at[target],
            recv_sem=recv_sem.at[source],
            device_id=(shard, target),
            device_id_type=pl.DeviceIdType.MESH,
        )

    def each(act):
        for step in range(1, tensor_count):
            target = lax.rem(me + step, tensor_count)
            for kind in (0, 1):

                @pl.when(takes(target) == kind)
                def _():
                    act(copy(kind, target, me))

    each(lambda c: c.start())
    for kind in (0, 1):

        @pl.when(takes(me) == kind)
        def _():
            local = pltpu.make_async_copy(
                looks[kind].at[me // 2], helds[kind].at[me], local_sem
            )
            local.start()
            local.wait()
            for step in range(1, tensor_count):
                other = lax.rem(me + step, tensor_count)
                copy(kind, other, other).wait_recv()

    each(lambda c: c.wait_send())


def deal_rows(look_square, look_wide, tensor_count):
    anywhere = pl.BlockSpec(memory_space=pl.ANY)
    return pl.pallas_call(
        functools.partial(deal, tensor_count // LAYERS, tensor_count),
        out_shape=tuple(
            jax.ShapeDtypeStruct((tensor_count,) + look.shape[1:], jnp.float32)
            for look in (look_square, look_wide)
        ),
        in_specs=[anywhere, anywhere],
        out_specs=(anywhere, anywhere),
        scratch_shapes=[
            pltpu.SemaphoreType.DMA,
            pltpu.SemaphoreType.DMA((tensor_count,)),
            pltpu.SemaphoreType.DMA((tensor_count,)),
        ],
        compiler_params=pltpu.CompilerParams(collective_id=1, has_side_effects=True),
    )(look_square, look_wide)


def shards(grad_square, grad_wide, moment_square, moment_wide):
    tensor_count = lax.axis_size("tensor")
    shard_count = lax.axis_size("shard")
    member = lax.axis_index("tensor")
    matrices, rows_square, width = grad_square.shape
    rows_wide = grad_wide.shape[1]
    flat_square = own_rows(grad_square, member, tensor_count).astype(jnp.float32)
    flat_wide = own_rows(grad_wide, member, tensor_count).astype(jnp.float32)
    new_square = momentum_decay * moment_square.reshape(flat_square.shape) + flat_square
    new_wide = momentum_decay * moment_wide.reshape(flat_wide.shape) + flat_wide
    look_square = flat_square + momentum_decay * new_square
    look_wide = flat_wide + momentum_decay * new_wide

    columns = tensor_count // LAYERS
    held_square, held_wide = deal_rows(look_square, look_wide, tensor_count)
    is_wide = (member // columns + member % columns) % 2 == 1
    current = jnp.where(
        is_wide,
        held_wide.reshape(rows_wide, width),
        jnp.pad(
            held_square.reshape(rows_square, width),
            ((0, rows_wide - rows_square), (0, 0)),
        ),
    )
    gram = summed_gram(current, shard_count)
    eye = jnp.eye(width, dtype=jnp.float32)
    total = jnp.sum(gram * eye)
    scale = 1.0 / (jnp.sqrt(total) + epsilon)
    gram = gram * (scale * scale)
    current = scale * current
    for iteration in range(ITERS):
        mixer = coef_b * gram + coef_c * dot(gram, gram)
        current = coef_a * current + dot(current, mixer)
        if iteration < ITERS - 1:
            mixed = coef_a * gram + dot(gram, mixer)
            gram = coef_a * mixed + dot(mixed, mixer)
    row_total = jnp.where(
        is_wide,
        math.sqrt(rows_wide * shard_count),
        math.sqrt(rows_square * shard_count),
    ).astype(jnp.float32)
    current = row_total * current

    update_square, update_wide = gather_rows(
        current, matrices, rows_square, rows_wide, tensor_count
    )
    return (
        update_square,
        update_wide,
        new_square.reshape(moment_square.shape),
        new_wide.reshape(moment_wide.shape),
    )


def solution(mesh):
    in_specs = (
        P(None, "shard", None),
        P(None, "shard", None),
        P(None, ("shard", "tensor")),
        P(None, ("shard", "tensor")),
    )
    return jax.shard_map(
        shards, mesh=mesh, in_specs=in_specs, out_specs=in_specs, check_vma=False
    )
```

```python
import functools
import math

import jax
import jax.numpy as jnp
from jax import lax
from jax.experimental import pallas as pl
from jax.experimental.pallas import tpu as pltpu
from jax.sharding import PartitionSpec as P

ITERS = 3
LAYERS = 4
CHUNKS = 4

coef_a = 3.4445
coef_b = -4.775
coef_c = 2.0315
momentum_decay = 0.95
epsilon = 1e-07


def dot(a, b):
    return jnp.dot(
        a, b, precision=lax.Precision.HIGH, preferred_element_type=jnp.float32
    )


def dot_rows(a, b):
    return lax.dot_general(
        a,
        b,
        (((0,), (0,)), ((), ())),
        precision=lax.Precision.HIGH,
        preferred_element_type=jnp.float32,
    )


def own_rows(grad, member, tensor_count):
    row_piece = grad.shape[1] // tensor_count
    return lax.dynamic_slice_in_dim(grad, member * row_piece, row_piece, 1)


def summed_gram(rows, shard_count):
    width = rows.shape[1]
    b = width // 3
    left, middle, right = rows[:, :b], rows[:, b : 2 * b], rows[:, 2 * b :]
    half_0 = dot_rows(left, rows)
    half_1 = jnp.concatenate(
        [dot_rows(middle, rows[:, b:]), dot_rows(right, right)], axis=1
    )
    first = lax.axis_index("shard") % 2 == 0
    across = [(i, i ^ 1) for i in range(shard_count)]
    kept = jnp.where(first, half_0, half_1)
    sent = jnp.where(first, half_1, half_0)
    pair = kept + lax.ppermute(sent, "shard", across)
    total = pair
    for hop in range(1, shard_count // 2):
        along = [(i, (i + 2 * hop) % shard_count) for i in range(shard_count)]
        total = total + lax.ppermute(pair, "shard", along)
    other = lax.ppermute(total, "shard", across)
    half_0 = jnp.where(first, total, other)
    half_1 = jnp.where(first, other, total)
    g01, g02 = half_0[:, b : 2 * b], half_0[:, 2 * b :]
    g12 = half_1[:, b : 2 * b]
    row_1 = jnp.concatenate([g01.T, half_1[:, : 2 * b]], axis=1)
    row_2 = jnp.concatenate([g02.T, g12.T, half_1[:, 2 * b :]], axis=1)
    return jnp.concatenate([half_0, row_1, row_2], axis=0)


def spread(layers, columns, x_ref, square_ref, wide_ref, local_sem, send_sem, recv_sem):
    me = lax.axis_index("tensor")
    shard = lax.axis_index("shard")
    layer = me // columns
    column = me % columns
    blocks = (square_ref, wide_ref)

    def device(to_layer, to_column):
        return (shard, to_layer * columns + to_column)

    def sideways(step):
        return lax.rem(column + step, columns)

    has_next = layer < layers - 1
    has_last = layer > 0
    barrier = pltpu.get_barrier_semaphore()

    def greet(target):
        pl.semaphore_signal(
            barrier, inc=1, device_id=target, device_id_type=pl.DeviceIdType.MESH
        )

    for step in range(1, columns):
        greet(device(layer, sideways(step)))

    @pl.when(has_next)
    def _():
        greet(device(layer + 1, column))

    @pl.when(has_last)
    def _():
        greet(device(layer - 1, column))

    pl.semaphore_wait(
        barrier, columns - 1 + has_next.astype(jnp.int32) + has_last.astype(jnp.int32)
    )

    def slot(kind, from_layer, from_column, chunk):
        block = blocks[kind]
        rows = block.shape[1] // CHUNKS
        return block.at[
            (from_layer * columns + from_column) // 2, pl.ds(chunk * rows, rows)
        ]

    def copy(kind, from_layer, from_column, chunk, way, target, source=None):
        place = slot(kind, from_layer, from_column, chunk)
        index = from_layer * columns + from_column
        return pltpu.make_async_remote_copy(
            src_ref=place if source is None else source,
            dst_ref=place,
            send_sem=send_sem.at[index, chunk, way],
            recv_sem=recv_sem.at[index, chunk],
            device_id=target,
            device_id_type=pl.DeviceIdType.MESH,
        )

    def routes(kind, distance, sign, chunk, act):
        origin = layer + sign * distance
        source = None
        if distance == 0:
            rows = blocks[kind].shape[1] // CHUNKS
            source = x_ref.at[pl.ds(chunk * rows, rows)]
        if distance == 0 or sign < 0:

            @pl.when(has_next)
            def _():
                act(copy(kind, origin, column, chunk, 0, device(layer + 1, column), source))

        if distance == 0 or sign > 0:

            @pl.when(has_last)
            def _():
                act(copy(kind, origin, column, chunk, 1, device(layer - 1, column), source))

        for step in range(1, columns):
            act(
                copy(
                    kind, origin, column, chunk, 1 + step,
                    device(layer, sideways(step)), source,
                )
            )

    def visit(act, arrive):
        for distance in range(layers):
            for kind in (0, 1):

                @pl.when(lax.rem(column + layer + distance, 2) == kind)
                def _():
                    for chunk in range(CHUNKS):
                        for sign in (-1, 1) if distance else (1,):
                            origin = layer + sign * distance

                            @pl.when((origin >= 0) & (origin < layers))
                            def _():
                                if distance and arrive:
                                    copy(
                                        kind, origin, column, chunk, 0,
                                        device(layer, sideways(1)),
                                    ).wait_recv()
                                routes(kind, distance, sign, chunk, act)

    visit(lambda c: c.start(), True)
    for kind in (0, 1):

        @pl.when(lax.rem(column + layer, 2) == kind)
        def _():
            block = blocks[kind]
            local = pltpu.make_async_copy(
                x_ref.at[pl.ds(0, block.shape[1])], block.at[me // 2], local_sem
            )
            local.start()
            local.wait()

    visit(lambda c: c.wait_send(), False)
    for origin in range(layers):
        for step in range(1, columns):
            for kind in (0, 1):

                @pl.when(lax.rem(sideways(step) + origin, 2) == kind)
                def _():
                    for chunk in range(CHUNKS):
                        copy(
                            kind, origin, sideways(step), chunk, 0,
                            device(layer, sideways(1)),
                        ).wait_recv()


def gather_rows(rows, matrices, rows_square, rows_wide, tensor_count):
    width = rows.shape[1]
    columns = tensor_count // LAYERS
    return pl.pallas_call(
        functools.partial(spread, LAYERS, columns),
        out_shape=(
            pltpu.VMEM((matrices, rows_square, width), jnp.float32),
            pltpu.VMEM((matrices, rows_wide, width), jnp.float32),
        ),
        in_specs=[pl.BlockSpec(memory_space=pl.ANY)],
        out_specs=(
            pl.BlockSpec(memory_space=pl.ANY),
            pl.BlockSpec(memory_space=pl.ANY),
        ),
        scratch_shapes=[
            pltpu.SemaphoreType.DMA,
            pltpu.SemaphoreType.DMA((tensor_count, CHUNKS, 1 + columns)),
            pltpu.SemaphoreType.DMA((tensor_count, CHUNKS)),
        ],
        compiler_params=pltpu.CompilerParams(collective_id=0, has_side_effects=True, vmem_limit_bytes=2**20),
    )(rows)


def deal(
    columns, tensor_count, look_square, look_wide, held_square, held_wide,
    local_sem, send_sem, recv_sem,
):
    me = lax.axis_index("tensor")
    shard = lax.axis_index("shard")
    looks = (look_square, look_wide)
    helds = (held_square, held_wide)
    barrier = pltpu.get_barrier_semaphore()

    def takes(member):
        return lax.rem(member // columns + lax.rem(member, columns), 2)

    for step in range(1, tensor_count):
        pl.semaphore_signal(
            barrier,
            inc=1,
            device_id=(shard, lax.rem(me + step, tensor_count)),
            device_id_type=pl.DeviceIdType.MESH,
        )
    pl.semaphore_wait(barrier, tensor_count - 1)

    def copy(kind, target, source):
        return pltpu.make_async_remote_copy(
            src_ref=looks[kind].at[target // 2],
            dst_ref=helds[kind].at[source],
            send_sem=send_sem.at[target],
            recv_sem=recv_sem.at[source],
            device_id=(shard, target),
            device_id_type=pl.DeviceIdType.MESH,
        )

    def each(act):
        for step in range(1, tensor_count):
            target = lax.rem(me + step, tensor_count)
            for kind in (0, 1):

                @pl.when(takes(target) == kind)
                def _():
                    act(copy(kind, target, me))

    each(lambda c: c.start())
    for kind in (0, 1):

        @pl.when(takes(me) == kind)
        def _():
            local = pltpu.make_async_copy(
                looks[kind].at[me // 2], helds[kind].at[me], local_sem
            )
            local.start()
            local.wait()
            for step in range(1, tensor_count):
                other = lax.rem(me + step, tensor_count)
                copy(kind, other, other).wait_recv()

    each(lambda c: c.wait_send())


def deal_rows(look_square, look_wide, tensor_count):
    anywhere = pl.BlockSpec(memory_space=pl.ANY)
    return pl.pallas_call(
        functools.partial(deal, tensor_count // LAYERS, tensor_count),
        out_shape=tuple(
            jax.ShapeDtypeStruct((tensor_count,) + look.shape[1:], jnp.float32)
            for look in (look_square, look_wide)
        ),
        in_specs=[anywhere, anywhere],
        out_specs=(anywhere, anywhere),
        scratch_shapes=[
            pltpu.SemaphoreType.DMA,
            pltpu.SemaphoreType.DMA((tensor_count,)),
            pltpu.SemaphoreType.DMA((tensor_count,)),
        ],
        compiler_params=pltpu.CompilerParams(collective_id=1, has_side_effects=True, vmem_limit_bytes=2**20),
    )(look_square, look_wide)


def shards(grad_square, grad_wide, moment_square, moment_wide):
    tensor_count = lax.axis_size("tensor")
    shard_count = lax.axis_size("shard")
    member = lax.axis_index("tensor")
    matrices, rows_square, width = grad_square.shape
    rows_wide = grad_wide.shape[1]
    flat_square = own_rows(grad_square, member, tensor_count).astype(jnp.float32)
    flat_wide = own_rows(grad_wide, member, tensor_count).astype(jnp.float32)
    new_square = momentum_decay * moment_square.reshape(flat_square.shape) + flat_square
    new_wide = momentum_decay * moment_wide.reshape(flat_wide.shape) + flat_wide
    look_square = flat_square + momentum_decay * new_square
    look_wide = flat_wide + momentum_decay * new_wide

    columns = tensor_count // LAYERS
    held_square, held_wide = deal_rows(look_square, look_wide, tensor_count)
    is_wide = (member // columns + member % columns) % 2 == 1
    current = jnp.where(
        is_wide,
        held_wide.reshape(rows_wide, width),
        jnp.pad(
            held_square.reshape(rows_square, width),
            ((0, rows_wide - rows_square), (0, 0)),
        ),
    )
    gram = summed_gram(current, shard_count)
    eye = jnp.eye(width, dtype=jnp.float32)
    total = jnp.sum(gram * eye)
    scale = 1.0 / (jnp.sqrt(total) + epsilon)
    gram = gram * (scale * scale)
    current = scale * current
    for iteration in range(ITERS):
        mixer = coef_b * gram + coef_c * dot(gram, gram)
        current = coef_a * current + dot(current, mixer)
        if iteration < ITERS - 1:
            mixed = coef_a * gram + dot(gram, mixer)
            gram = coef_a * mixed + dot(mixed, mixer)
    row_total = jnp.where(
        is_wide,
        math.sqrt(rows_wide * shard_count),
        math.sqrt(rows_square * shard_count),
    ).astype(jnp.float32)
    current = row_total * current

    update_square, update_wide = gather_rows(
        current, matrices, rows_square, rows_wide, tensor_count
    )
    return (
        update_square,
        update_wide,
        new_square.reshape(moment_square.shape),
        new_wide.reshape(moment_wide.shape),
    )


def solution(mesh):
    in_specs = (
        P(None, "shard", None),
        P(None, "shard", None),
        P(None, ("shard", "tensor")),
        P(None, ("shard", "tensor")),
    )
    return jax.shard_map(
        shards, mesh=mesh, in_specs=in_specs, out_specs=in_specs, check_vma=False
    )
```
